512 devices in a mesh: section: 8 (over x, y_hi), seq: 64 (over y_lo, z, core).
Axes of the slice: x: 4, y: 8 (y_hi: 2, y_lo: 4; y = y_hi * 4 + y_lo), z: 8, core: 2. Of those that a mesh axis runs over, the one named last changes fastest.
Arguments:
- hidden: bfloat16 [8, 2, 4096, 2048], P('section', None, 'seq'), may hold values from -16 to 16
- queries: bfloat16 [8, 2, 4096, 1024], P('section', None, 'seq'), may hold values from -6 to 6
- keys_values: bfloat16 [8, 2, 4096, 512], P('section', None, 'seq'), may hold values from -6 to 6
- out_grad: bfloat16 [8, 2, 4096, 2048], P('section', None, 'seq'), may hold values from -96 to 96
- qkv_weight: bfloat16 [8, 2048, 1536], P('section', 'seq'), may hold values from -0.125 to 0.125
- out_weight: bfloat16 [8, 2048, 1024], P('section', 'seq'), may hold values from -0.1875 to 0.1875
- adapter_down_maps: bfloat16 [8, 2048, 128], P('section', 'seq'), may hold values from -0.125 to 0.125
- adapter_up_maps: bfloat16 [8, 64, 1280], P('section'), may hold values from -0.119628906 to 0.119628906
Outputs:
- passed_grad: bfloat16 [8, 2, 4096, 2048], P('section', None, 'seq')
- a_grad: float32 [8, 2048, 128], P('section', 'seq')
- b_grad: float32 [8, 64, 1280], P('section', None, 'seq')
The draws below stay inside these ranges and needn't reach their ends.
All inputs are finite; a program needn't handle non-finite values.
Results may differ from the reference program's by a relative error of at most 0.0071.
Values may be sent and summed in bfloat16 or wider, within the bound.
No kernel may reach another device: no remote copies, remote signals or barrier semaphores. Data moves between devices by JAX's collectives and lax.ppermute only.
A program may use at most 64 MiB of HBM per device.

```python
import jax
import jax.numpy as jnp
from jax import lax

MODEL_WIDTH = 2048
QUERY_HEADS = 16
KEY_VALUE_HEADS = 4
HEAD_SIZE = 64
ADAPTER_RANK = 64
ADAPTER_NUMER = 128
GRADIENT_SCALE = 32
SEQS = 2
RELAY_SECTIONS = 8
LEN = 4096


def draw_queries(key, part):
    key = jax.random.fold_in(key, 1)
    shape = (RELAY_SECTIONS, SEQS, LEN, QUERY_HEADS * HEAD_SIZE)
    values = jax.random.truncated_normal(key, -6.0, 6.0, shape, jnp.float32)
    return values.astype(jnp.bfloat16)


def draw_keys_values(key, part):
    key = jax.random.fold_in(key, 2)
    shape = (RELAY_SECTIONS, SEQS, LEN, 2 * KEY_VALUE_HEADS * HEAD_SIZE)
    values = jax.random.truncated_normal(key, -6.0, 6.0, shape, jnp.float32)
    return values.astype(jnp.bfloat16)


def raised(values, stream_key, source, target, shards_of, factor):
    def block_of(axis_at):
        return (jnp.arange(values.shape[axis_at]) // (values.shape[axis_at] // shards_of)).reshape((-1,) + (1,) * (values.ndim - 1 - axis_at))

    first = jax.random.permutation(stream_key, shards_of)[block_of(target)]
    other_side = (block_of(target) + shards_of // 2) % shards_of
    return jnp.where((block_of(source) == first) | (block_of(source) == other_side), factor * values, values)


def block_levels(own_key, shape, shards, smallest, largest):
    def one(dim, parts):
        heights = jax.random.uniform(jax.random.fold_in(jax.random.fold_in(own_key, 6), dim), (parts,), jnp.float32, smallest / len(shards), largest / len(shards))
        return jnp.repeat(jnp.exp(heights), shape[dim] // parts).reshape((-1,) + (1,) * (len(shape) - dim - 1))

    level = one(*shards[0])
    for cut in shards[1:]:
        level = level * one(*cut)
    return level


def noise(stream_key, dims, deviation, reach, shards=(), kind=jnp.bfloat16):
    entries = jax.random.normal(stream_key, dims, jnp.float32) * deviation
    if len(shards) > 0:
        entries = block_levels(stream_key, dims, shards, -0.22, 0.18) * entries
    return jnp.clip(entries, min=-reach, max=reach).astype(kind)


def heavy_noise(stream_key, shape, spread, most, cuts, heavy, held_as=jnp.bfloat16):
    values = spread * jax.random.normal(stream_key, shape, jnp.float32)
    if cuts:
        values = values * block_levels(stream_key, shape, cuts, -0.22, 0.18)
    return jnp.clip(raised(values, jax.random.fold_in(stream_key, 3), *heavy), -most, most).astype(held_as)


def setup_inputs(seed: int = 0) -> dict:
    seeds = jax.random.split(jax.random.key(seed), 9)
    hidden = heavy_noise(seeds[0], (RELAY_SECTIONS, SEQS, LEN, MODEL_WIDTH), 1.0, 16.0, ((0, 8), (2, 64)), (2, 3, 64, 4.0))
    queries = draw_queries(jax.random.fold_in(seeds[8], 71), 0)
    keys_values = draw_keys_values(jax.random.fold_in(seeds[8], 71), 0)
    out_grad = noise(seeds[3], (RELAY_SECTIONS, SEQS, LEN, MODEL_WIDTH), 16.0, 96.0, ((0, 8), (2, 64)))
    qkv_weight = noise(seeds[4], (RELAY_SECTIONS, MODEL_WIDTH, (QUERY_HEADS + 2 * KEY_VALUE_HEADS) * HEAD_SIZE), MODEL_WIDTH ** -0.5, 0.125, ((0, 8), (1, 64)))
    out_weight = noise(seeds[5], (RELAY_SECTIONS, MODEL_WIDTH, QUERY_HEADS * HEAD_SIZE), (QUERY_HEADS * HEAD_SIZE) ** -0.5, 0.1875, ((0, 8), (1, 64)))
    adapter_down_maps = noise(seeds[6], (RELAY_SECTIONS, MODEL_WIDTH, 2 * ADAPTER_RANK), MODEL_WIDTH ** -0.5, 0.125, ((0, 8), (1, 64)))
    adapter_up_maps = noise(seeds[7], (RELAY_SECTIONS, ADAPTER_RANK, (QUERY_HEADS + KEY_VALUE_HEADS) * HEAD_SIZE), 0.02, 0.119628906, ((0, 8),))
    return dict(hidden=hidden, queries=queries, keys_values=keys_values, out_grad=out_grad, qkv_weight=qkv_weight, out_weight=out_weight, adapter_down_maps=adapter_down_maps, adapter_up_maps=adapter_up_maps)


def head_grads(query_h, grad_h, key_h, value_h):
    position = jnp.arange(LEN)
    causal = position[:, None] >= position[None, :]
    score_scale = HEAD_SIZE ** -0.5
    scores = jnp.dot(query_h, key_h.T, preferred_element_type=jnp.float32) * score_scale
    scores = jnp.where(causal, scores, -jnp.inf)
    row_max = jnp.max(scores, axis=1, keepdims=True)
    exponent = jnp.exp(scores - row_max)
    attn_prob = exponent / jnp.sum(exponent, axis=1, keepdims=True)
    prob_grad = jnp.dot(grad_h, value_h.T, preferred_element_type=jnp.float32)
    row_delta = jnp.sum(attn_prob * prob_grad, axis=1, keepdims=True)
    score_grad = (attn_prob * (prob_grad - row_delta) * score_scale).astype(jnp.bfloat16)
    prob_half = attn_prob.astype(jnp.bfloat16)
    query_gradient = jnp.dot(score_grad, key_h, preferred_element_type=jnp.float32)
    key_grad = jnp.dot(score_grad.T, query_h, preferred_element_type=jnp.float32)
    value_gradient = jnp.dot(prob_half.T, grad_h, preferred_element_type=jnp.float32)
    return query_gradient.astype(jnp.bfloat16), key_grad, value_gradient


def section_grads(operands):
    hidden, queries, keys_values, out_grad, qkv_weight, out_weight, adapter_down_maps, adapter_up_maps = operands
    tokens = SEQS * LEN
    group_q = QUERY_HEADS // KEY_VALUE_HEADS
    q_cols = QUERY_HEADS * HEAD_SIZE
    attn_grad = jnp.dot(out_grad.reshape(tokens, MODEL_WIDTH), out_weight, preferred_element_type=jnp.float32).astype(jnp.bfloat16)
    query_groups = queries.reshape(SEQS, LEN, KEY_VALUE_HEADS, group_q, HEAD_SIZE).transpose(0, 2, 3, 1, 4).reshape(SEQS * KEY_VALUE_HEADS, group_q, LEN, HEAD_SIZE)
    grad_groups = attn_grad.reshape(SEQS, LEN, KEY_VALUE_HEADS, group_q, HEAD_SIZE).transpose(0, 2, 3, 1, 4).reshape(SEQS * KEY_VALUE_HEADS, group_q, LEN, HEAD_SIZE)
    kv_groups = keys_values.reshape(SEQS, LEN, KEY_VALUE_HEADS, 2, HEAD_SIZE).transpose(0, 2, 3, 1, 4).reshape(SEQS * KEY_VALUE_HEADS, 2, LEN, HEAD_SIZE)

    def one_group(items):
        query_set, grad_set, kv_set = items
        key_sum = jnp.zeros((LEN, HEAD_SIZE), jnp.float32)
        value_sum = jnp.zeros((LEN, HEAD_SIZE), jnp.float32)
        query_list = []
        for member in range(group_q):
            query_part, key_part, value_part = head_grads(query_set[member], grad_set[member], kv_set[0], kv_set[1])
            query_list.append(query_part)
            key_sum = key_sum + key_part
            value_sum = value_sum + value_part
        return jnp.stack(query_list), jnp.stack([key_sum, value_sum]).astype(jnp.bfloat16)

    query_gradient, kv_grad = lax.map(one_group, (query_groups, grad_groups, kv_groups))
    query_gradient = query_gradient.reshape(SEQS, KEY_VALUE_HEADS, group_q, LEN, HEAD_SIZE).transpose(0, 3, 1, 2, 4).reshape(tokens, q_cols)
    kv_grad = kv_grad.reshape(SEQS, KEY_VALUE_HEADS, 2, LEN, HEAD_SIZE).transpose(2, 0, 3, 1, 4).reshape(2, tokens, KEY_VALUE_HEADS * HEAD_SIZE)
    key_grad = kv_grad[0]
    value_gradient = kv_grad[1]
    grad_qkv = jnp.concatenate([query_gradient, key_grad, value_gradient], axis=1)
    hidden_rows = hidden.reshape(tokens, MODEL_WIDTH)
    adapter_between = jnp.concatenate([
        jnp.dot(query_gradient, adapter_up_maps[:, :q_cols].T, preferred_element_type=jnp.float32),
        jnp.dot(value_gradient, adapter_up_maps[:, q_cols:].T, preferred_element_type=jnp.float32)], axis=1).astype(jnp.bfloat16)
    adapter_scale = ADAPTER_NUMER / ADAPTER_RANK
    input_gradient = jnp.dot(grad_qkv, qkv_weight.T, preferred_element_type=jnp.float32)
    input_gradient = input_gradient + adapter_scale * jnp.dot(adapter_between, adapter_down_maps.T, preferred_element_type=jnp.float32)
    input_gradient = input_gradient.astype(jnp.bfloat16).reshape(SEQS, LEN, MODEL_WIDTH)
    adapter_reduced = jnp.dot(hidden_rows, adapter_down_maps, preferred_element_type=jnp.float32).astype(jnp.bfloat16)
    scale_factor = adapter_scale / GRADIENT_SCALE
    a_grad = scale_factor * jnp.dot(hidden_rows.T, adapter_between, preferred_element_type=jnp.float32)
    b_grad = scale_factor * jnp.concatenate([
        jnp.dot(adapter_reduced[:, :ADAPTER_RANK].T, query_gradient, preferred_element_type=jnp.float32),
        jnp.dot(adapter_reduced[:, ADAPTER_RANK:].T, value_gradient, preferred_element_type=jnp.float32)], axis=1)
    return input_gradient, a_grad, b_grad


def reference(hidden, queries, keys_values, out_grad, qkv_weight, out_weight, adapter_down_maps, adapter_up_maps):
    input_gradient, a_grad, b_grad = lax.map(section_grads, (hidden, queries, keys_values, out_grad, qkv_weight, out_weight, adapter_down_maps, adapter_up_maps))
    passed_grad = jnp.roll(input_gradient, -1, axis=0)
    return passed_grad, a_grad, b_grad
```

```python
import jax
import jax.numpy as jnp
from jax import lax
from jax.experimental import pallas as pl
from jax.experimental.pallas import tpu as pltpu
from jax.sharding import Mesh, PartitionSpec as P

MODEL_WIDTH = 2048
QUERY_HEADS = 16
KEY_VALUE_HEADS = 4
HEAD_SIZE = 64
ADAPTER_RANK = 64
ADAPTER_NUMER = 128
GRADIENT_SCALE = 32
SEQS = 2
LEN = 4096

LINE = 4
RING = 8
CORES = 2
SEQ_AXES = ("y", "z", "core")
DEVICES = LINE * RING * CORES
PER_SEQ = LEN // DEVICES
Q_COLS = QUERY_HEADS * HEAD_SIZE
KV_COLS = 2 * HEAD_SIZE
GROUP = QUERY_HEADS // KEY_VALUE_HEADS
GROUP_WIDTH = GROUP * HEAD_SIZE
PAIR_WIDTH = CORES * GROUP_WIDTH

CHUNK = CORES * PER_SEQ
SPAN = RING * CHUNK
COLS = GROUP * CHUNK
TILE = SPAN
TILES = LEN // TILE
EXP_SCALE = HEAD_SIZE ** (-0.5) * 1.4426950408889634


def dot(a, b):
    return jnp.dot(a, b, preferred_element_type=jnp.float32)


def head_columns(rows):
    turned = rows.astype(jnp.float32).T
    return jnp.concatenate(
        [turned[h * HEAD_SIZE : (h + 1) * HEAD_SIZE] for h in range(GROUP)], axis=1
    )


def causal(scores, first_key, first_row):
    key_pos = first_key + lax.broadcasted_iota(jnp.int32, scores.shape, 0)
    row_pos = first_row + lax.broadcasted_iota(jnp.int32, scores.shape, 1) % CHUNK
    return jnp.where(row_pos >= key_pos, scores, -jnp.inf)


def forward_kernel(part_ref, query_ref, kv_ref, turned_ref, out_ref, log_ref):
    part = part_ref[0]

    def chunk(j, carry):
        first_row = j * SPAN + part * CHUNK
        columns = head_columns(query_ref[j])
        query_cols = jnp.concatenate([columns, jnp.zeros_like(columns)], axis=0).astype(
            jnp.bfloat16
        )

        def tile(t, state, masked):
            top, total, mixed = state
            scores = dot(kv_ref[t], query_cols)
            if masked:
                scores = causal(scores, t * TILE, first_row)
            new_top = jnp.maximum(top, jnp.max(scores, axis=0, keepdims=True))
            shrink = jnp.exp2((top - new_top) * EXP_SCALE)
            power = jnp.exp2(scores * EXP_SCALE - new_top * EXP_SCALE)
            total = total * shrink + jnp.sum(power, axis=0, keepdims=True)
            mixed = mixed * shrink + dot(turned_ref[t, HEAD_SIZE:], power.astype(jnp.bfloat16))
            return new_top, total, mixed

        state = (
            jnp.full((1, COLS), -jnp.inf, jnp.float32),
            jnp.zeros((1, COLS), jnp.float32),
            jnp.zeros((HEAD_SIZE, COLS), jnp.float32),
        )
        last = first_row // TILE
        state = lax.fori_loop(0, last, lambda t, s: tile(t, s, False), state)
        top, total, mixed = tile(last, state, True)
        out_ref[j] = mixed / total
        log_ref[j] = top * EXP_SCALE + jnp.log2(total)
        return carry

    lax.fori_loop(0, LINE, chunk, 0)


def backward_kernel(
    part_ref, query_ref, grad_ref, kv_ref, turned_ref, out_ref, log_ref, dq_ref, dkv_ref, acc_ref
):
    part = part_ref[0]
    scale = HEAD_SIZE ** (-0.5)
    acc_ref[...] = jnp.zeros_like(acc_ref)

    def chunk(j, carry):
        first_row = j * SPAN + part * CHUNK
        query_half = head_columns(query_ref[j])
        grad_half = head_columns(grad_ref[j])
        blank = jnp.zeros_like(query_half)
        query_full = jnp.concatenate([query_half, blank], axis=0)
        grad_full = jnp.concatenate([blank, grad_half], axis=0)
        query_cols = query_full.astype(jnp.bfloat16)
        grad_cols = grad_full.astype(jnp.bfloat16)
        query_rows = query_full.T.astype(jnp.bfloat16)
        grad_rows = grad_full.T.astype(jnp.bfloat16)
        delta = jnp.sum(grad_half * out_ref[j], axis=0, keepdims=True)
        log_total = log_ref[j]

        def tile(t, query_sum, masked):
            pair = kv_ref[t]
            scores = dot(pair, query_cols)
            if masked:
                scores = causal(scores, t * TILE, first_row)
            prob = jnp.exp2(scores * EXP_SCALE - log_total)
            prob_grad = dot(pair, grad_cols)
            score_grad = (prob * (prob_grad - delta)).astype(jnp.bfloat16)
            acc_ref[t] += dot(score_grad, query_rows) + dot(prob.astype(jnp.bfloat16), grad_rows)
            return query_sum + dot(turned_ref[t, :HEAD_SIZE], score_grad)

        last = first_row // TILE
        query_sum = lax.fori_loop(
            0, last, lambda t, s: tile(t, s, False), jnp.zeros((HEAD_SIZE, COLS), jnp.float32)
        )
        query_sum = tile(last, query_sum, True) * scale
        stacked = jnp.concatenate(
            [query_sum[:, h * CHUNK : (h + 1) * CHUNK] for h in range(GROUP)], axis=0
        )
        dq_ref[j] = stacked.T.astype(jnp.bfloat16)
        return carry

    lax.fori_loop(0, LINE, chunk, 0)
    lane = lax.broadcasted_iota(jnp.int32, acc_ref.shape, 2)
    dkv_ref[...] = (acc_ref[...] * jnp.where(lane < HEAD_SIZE, scale, 1.0)).astype(jnp.bfloat16)


VMEM = pl.BlockSpec(memory_space=pltpu.VMEM)
SMEM = pl.BlockSpec(memory_space=pltpu.SMEM)
PARAMS = pltpu.CompilerParams(vmem_limit_bytes=48 * 2**20)


def attend_forward(part, query, kv, turned):
    return pl.pallas_call(
        forward_kernel,
        out_shape=(
            jax.ShapeDtypeStruct((LINE, HEAD_SIZE, COLS), jnp.float32),
            jax.ShapeDtypeStruct((LINE, 1, COLS), jnp.float32),
        ),
        in_specs=[SMEM, VMEM, VMEM, VMEM],
        out_specs=(VMEM, VMEM),
        compiler_params=PARAMS,
        name="attention_forward",
    )(part, query, kv, turned)


def attend_backward(part, query, grad, kv, turned, out, log_total):
    return pl.pallas_call(
        backward_kernel,
        out_shape=(
            jax.ShapeDtypeStruct((LINE, CHUNK, GROUP_WIDTH), jnp.bfloat16),
            jax.ShapeDtypeStruct((TILES, TILE, KV_COLS), jnp.bfloat16),
        ),
        in_specs=[SMEM] + [VMEM] * 6,
        out_specs=(VMEM, VMEM),
        scratch_shapes=[pltpu.VMEM((TILES, TILE, KV_COLS), jnp.float32)],
        compiler_params=PARAMS,
        name="attention_backward",
    )(part, query, grad, kv, turned, out, log_total)


def exchange(blocks, axes):
    return lax.all_to_all(blocks, axes, split_axis=0, concat_axis=0, tiled=True)


def swap(block):
    return lax.ppermute(block, "core", [(0, 1), (1, 0)])


def contract(a, b, dims):
    return lax.dot_general(a, b, (dims, ((), ())), preferred_element_type=jnp.float32)


def per_device(
    hidden,
    queries,
    keys_values,
    out_grad,
    qkv_weight,
    out_weight,
    adapter_down_maps,
    adapter_up_maps,
):
    ring_at = lax.axis_index("z")
    core = lax.axis_index("core")
    part = ring_at.astype(jnp.int32).reshape(1)
    tokens = SEQS * PER_SEQ
    halves = LINE // SEQS
    weight_rows = MODEL_WIDTH // DEVICES

    gathered = lax.all_gather(
        jnp.concatenate([qkv_weight[0], adapter_down_maps[0]], axis=1),
        SEQ_AXES,
        axis=0,
        tiled=True,
    )
    weight_all = gathered[:, : Q_COLS + 2 * KEY_VALUE_HEADS * HEAD_SIZE]
    down_all = gathered[:, Q_COLS + 2 * KEY_VALUE_HEADS * HEAD_SIZE :]

    grad_part = jnp.broadcast_to(
        out_grad[0][:, None], (SEQS, halves, PER_SEQ, MODEL_WIDTH)
    )
    query_part = (
        queries[0].reshape(SEQS, PER_SEQ, halves, PAIR_WIDTH).transpose(0, 2, 1, 3)
    )
    row_send = jnp.concatenate([grad_part, query_part], axis=3).reshape(
        LINE, PER_SEQ, MODEL_WIDTH + PAIR_WIDTH
    )
    row_own = exchange(row_send, ("y",))
    row_other = swap(row_own)
    first = jnp.where(core == 0, row_own, row_other)
    second = jnp.where(core == 0, row_other, row_own)
    rows = jnp.stack([first, second], axis=1).reshape(
        LINE * CHUNK, MODEL_WIDTH + PAIR_WIDTH
    )
    grad_rows = rows[:, :MODEL_WIDTH]
    query_pair = rows[:, MODEL_WIDTH:]
    query_rows = jnp.where(
        core == 0, query_pair[:, :GROUP_WIDTH], query_pair[:, GROUP_WIDTH:]
    ).reshape(LINE, CHUNK, GROUP_WIDTH)

    kv_part = keys_values[0].reshape(SEQS, PER_SEQ, halves, CORES, KV_COLS).transpose(0, 2, 3, 1, 4)
    kv_send = jnp.broadcast_to(
        kv_part[:, :, None], (SEQS, halves, RING, CORES, PER_SEQ, KV_COLS)
    ).reshape(DEVICES, PER_SEQ, KV_COLS)
    kv = exchange(kv_send, SEQ_AXES).reshape(TILES, TILE, KV_COLS)
    turned = kv.transpose(0, 2, 1)
    out_part = (
        out_weight[0].reshape(weight_rows, halves, CORES, GROUP_WIDTH).transpose(1, 2, 0, 3)
    )
    out_send = jnp.broadcast_to(
        out_part[None, :, None], (SEQS, halves, RING, CORES, weight_rows, GROUP_WIDTH)
    ).reshape(DEVICES, weight_rows, GROUP_WIDTH)
    out_all = exchange(out_send, SEQ_AXES).reshape(MODEL_WIDTH, GROUP_WIDTH)

    attn_out, log_total = attend_forward(part, query_rows, kv, turned)
    attn_grad = dot(grad_rows, out_all).astype(jnp.bfloat16).reshape(LINE, CHUNK, GROUP_WIDTH)
    query_gradient, kv_grad = attend_backward(
        part, query_rows, attn_grad, kv, turned, attn_out, log_total
    )

    query_back = exchange(
        query_gradient.reshape(LINE * CORES, PER_SEQ, GROUP_WIDTH), ("y", "core")
    )
    kv_back = exchange(kv_grad.reshape(DEVICES, PER_SEQ, KV_COLS), SEQ_AXES)
    query_local = (
        query_back.reshape(SEQS, halves * CORES, PER_SEQ, GROUP_WIDTH)
        .transpose(0, 2, 1, 3)
        .reshape(tokens, Q_COLS)
    )
    kv_local = (
        jnp.sum(
            kv_back.reshape(SEQS, halves, RING, CORES, PER_SEQ, KV_COLS).astype(jnp.float32), axis=2
        )
        .astype(jnp.bfloat16)
        .reshape(SEQS, KEY_VALUE_HEADS, PER_SEQ, 2, HEAD_SIZE)
        .transpose(0, 2, 3, 1, 4)
        .reshape(tokens, 2 * KEY_VALUE_HEADS * HEAD_SIZE)
    )
    grad_qkv = jnp.concatenate([query_local, kv_local], axis=1)
    value_local = kv_local[:, KEY_VALUE_HEADS * HEAD_SIZE :]
    up_maps = adapter_up_maps[0]
    adapter_between = jnp.concatenate(
        [
            contract(query_local, up_maps[:, :Q_COLS], ((1,), (1,))),
            contract(value_local, up_maps[:, Q_COLS:], ((1,), (1,))),
        ],
        axis=1,
    ).astype(jnp.bfloat16)
    adapter_scale = ADAPTER_NUMER / ADAPTER_RANK
    input_gradient = contract(grad_qkv, weight_all, ((1,), (1,)))
    input_gradient = input_gradient + adapter_scale * contract(
        adapter_between, down_all, ((1,), (1,))
    )
    input_gradient = input_gradient.astype(jnp.bfloat16).reshape(1, SEQS, PER_SEQ, MODEL_WIDTH)
    sections = lax.axis_size("section")
    passed = lax.ppermute(
        input_gradient, "section", [((i + 1) % sections, i) for i in range(sections)]
    )

    hidden_rows = hidden[0].reshape(tokens, MODEL_WIDTH)
    adapter_reduced = dot(hidden_rows, down_all).astype(jnp.bfloat16)
    a_term = contract(hidden_rows, adapter_between, ((0,), (0,)))
    b_term = jnp.concatenate(
        [
            contract(adapter_reduced[:, :ADAPTER_RANK], query_local, ((0,), (0,))),
            contract(adapter_reduced[:, ADAPTER_RANK:], value_local, ((0,), (0,))),
        ],
        axis=1,
    )
    b_cols = b_term.shape[1] // DEVICES
    a_send = a_term.astype(jnp.bfloat16).reshape(DEVICES, weight_rows * 2 * ADAPTER_RANK)
    b_send = (
        b_term.astype(jnp.bfloat16)
        .reshape(ADAPTER_RANK, DEVICES, b_cols)
        .transpose(1, 0, 2)
        .reshape(DEVICES, ADAPTER_RANK * b_cols)
    )
    terms = exchange(jnp.concatenate([a_send, b_send], axis=1), SEQ_AXES)
    sums = (adapter_scale / GRADIENT_SCALE) * jnp.sum(terms.astype(jnp.float32), axis=0)
    a_sum = sums[: a_send.shape[1]].reshape(1, weight_rows, 2 * ADAPTER_RANK)
    b_sum = sums[a_send.shape[1] :].reshape(1, ADAPTER_RANK, b_cols)
    return (passed, a_sum, b_sum)


def solution(mesh):
    sections = mesh.shape["section"]
    fine = Mesh(mesh.devices.reshape(sections, LINE, RING, CORES), ("section",) + SEQ_AXES)
    return jax.shard_map(
        per_device,
        mesh=fine,
        in_specs=(
            P("section", None, SEQ_AXES, None),
            P("section", None, SEQ_AXES, None),
            P("section", None, SEQ_AXES, None),
            P("section", None, SEQ_AXES, None),
            P("section", SEQ_AXES, None),
            P("section", SEQ_AXES, None),
            P("section", SEQ_AXES, None),
            P("section", None, None),
        ),
        out_specs=(
            P("section", None, SEQ_AXES, None),
            P("section", SEQ_AXES, None),
            P("section", None, SEQ_AXES),
        ),
        check_vma=False,
    )
```

```python
import jax
import jax.numpy as jnp
from jax import lax
from jax.experimental import pallas as pl
from jax.experimental.pallas import tpu as pltpu
from jax.sharding import Mesh, PartitionSpec as P

MODEL_WIDTH = 2048
QUERY_HEADS = 16
KEY_VALUE_HEADS = 4
HEAD_SIZE = 64
ADAPTER_RANK = 64
ADAPTER_NUMER = 128
GRADIENT_SCALE = 32
SEQS = 2
LEN = 4096

LINE = 4
RING = 8
CORES = 2
SEQ_AXES = ("y", "z", "core")
DEVICES = LINE * RING * CORES
PER_SEQ = LEN // DEVICES
Q_COLS = QUERY_HEADS * HEAD_SIZE
KV_COLS = 2 * HEAD_SIZE
GROUP = QUERY_HEADS // KEY_VALUE_HEADS
GROUP_WIDTH = GROUP * HEAD_SIZE
PAIR_WIDTH = CORES * GROUP_WIDTH
WEIGHT_ROWS = MODEL_WIDTH // DEVICES
B_ROWS = (QUERY_HEADS + KEY_VALUE_HEADS) * HEAD_SIZE // DEVICES // 2
ADAPTER_SCALE = ADAPTER_NUMER / ADAPTER_RANK
TERM_SCALE = ADAPTER_SCALE / GRADIENT_SCALE
ROW_COLS = MODEL_WIDTH + PAIR_WIDTH
WEIGHT_COLS = Q_COLS + 2 * KEY_VALUE_HEADS * HEAD_SIZE + 2 * ADAPTER_RANK
FOLD = 896

CHUNK = CORES * PER_SEQ
SPAN = RING * CHUNK
COLS = GROUP * CHUNK
TILE = SPAN
EXP_SCALE = HEAD_SIZE ** (-0.5) * 1.4426950408889634


def dot(a, b):
    return jnp.dot(a, b, preferred_element_type=jnp.float32)


def contract(a, b, dims):
    return lax.dot_general(a, b, (dims, ((), ())), preferred_element_type=jnp.float32)


def head_columns(rows):
    turned = rows.astype(jnp.float32).T
    return jnp.concatenate(
        [turned[h * HEAD_SIZE : (h + 1) * HEAD_SIZE] for h in range(GROUP)], axis=1
    )


def causal_mask(part, core):
    key_pos = lax.broadcasted_iota(jnp.int32, (TILE, COLS), 0)
    row = lax.broadcasted_iota(jnp.int32, (TILE, COLS), 1) % CHUNK
    row_pos = part * CHUNK + (row + core * PER_SEQ) % CHUNK
    return row_pos >= key_pos


def tile_of(pair_ref, t):
    return pair_ref[:, t, :, :PER_SEQ, :].reshape(TILE, KV_COLS)


def query_rows_of(own_ref, other_ref, j, core):
    columns = pl.ds(pl.multiple_of(MODEL_WIDTH + core * GROUP_WIDTH, GROUP_WIDTH), GROUP_WIDTH)
    return jnp.concatenate([own_ref[j, :, columns], other_ref[j, :, columns]], axis=0)


def attention_kernel(
    place_ref, own_ref, other_ref, pair_ref, dq_ref, dkv_ref, acc_ref, turned_ref, weight_ref
):
    part, core = place_ref[0], place_ref[1]
    scale = HEAD_SIZE ** (-0.5)
    acc_ref[...] = jnp.zeros_like(acc_ref)

    def prepare(t, carry):
        turned_ref[t] = tile_of(pair_ref, t).T
        for z in range(RING):
            for c in range(CORES):
                block = pair_ref[z, t, c, PER_SEQ:, :]
                weight_ref[t, z, c] = jnp.concatenate(
                    [block[:WEIGHT_ROWS], block[WEIGHT_ROWS:]], axis=1
                )
        return carry

    lax.fori_loop(0, LINE, prepare, 0)
    weight = weight_ref[...].reshape(MODEL_WIDTH, GROUP_WIDTH)

    def chunk(j, carry):
        query_half = head_columns(query_rows_of(own_ref, other_ref, j, core))
        out_grad = jnp.concatenate(
            [own_ref[j, :, :MODEL_WIDTH], other_ref[j, :, :MODEL_WIDTH]], axis=0
        )
        grad_half = head_columns(dot(out_grad, weight).astype(jnp.bfloat16))
        blank = jnp.zeros_like(query_half)
        query_full = jnp.concatenate([query_half, blank], axis=0)
        grad_full = jnp.concatenate([blank, grad_half], axis=0)
        query_cols = query_full.astype(jnp.bfloat16)
        grad_cols = grad_full.astype(jnp.bfloat16)
        query_rows = query_full.T.astype(jnp.bfloat16)
        grad_rows = grad_full.T.astype(jnp.bfloat16)

        def scores_of(t, masked):
            scores = dot(tile_of(pair_ref, t), query_cols)
            if masked:
                scores = jnp.where(causal_mask(part, core), scores, -jnp.inf)
            return scores

        def forward_tile(t, state, masked):
            top, total, mixed = state
            scores = scores_of(t, masked)
            new_top = jnp.maximum(top, jnp.max(scores, axis=0, keepdims=True))
            shrink = jnp.exp2((top - new_top) * EXP_SCALE)
            power = jnp.exp2(scores * EXP_SCALE - new_top * EXP_SCALE)
            total = total * shrink + jnp.sum(power, axis=0, keepdims=True)
            mixed = mixed * shrink + dot(turned_ref[t, HEAD_SIZE:], power.astype(jnp.bfloat16))
            return new_top, total, mixed

        state = (
            jnp.full((1, COLS), -jnp.inf, jnp.float32),
            jnp.zeros((1, COLS), jnp.float32),
            jnp.zeros((HEAD_SIZE, COLS), jnp.float32),
        )
        state = lax.fori_loop(0, j, lambda t, s: forward_tile(t, s, False), state)
        top, total, mixed = forward_tile(j, state, True)
        delta = jnp.sum(grad_half * (mixed / total), axis=0, keepdims=True)
        log_total = top * EXP_SCALE + jnp.log2(total)

        def backward_tile(t, query_sum, masked):
            prob = jnp.exp2(scores_of(t, masked) * EXP_SCALE - log_total)
            prob_grad = dot(tile_of(pair_ref, t), grad_cols)
            score_grad = (prob * (prob_grad - delta)).astype(jnp.bfloat16)
            acc_ref[t] += dot(score_grad, query_rows) + dot(prob.astype(jnp.bfloat16), grad_rows)
            return query_sum + dot(turned_ref[t, :HEAD_SIZE], score_grad)

        query_sum = lax.fori_loop(
            0,
            j,
            lambda t, s: backward_tile(t, s, False),
            jnp.zeros((HEAD_SIZE, COLS), jnp.float32),
        )
        query_sum = backward_tile(j, query_sum, True) * scale
        stacked = jnp.concatenate(
            [query_sum[:, h * CHUNK : (h + 1) * CHUNK] for h in range(GROUP)], axis=0
        )
        dq_ref[j] = stacked.T.astype(jnp.bfloat16).reshape(CORES, PER_SEQ, GROUP_WIDTH)
        return carry

    lax.fori_loop(0, LINE, chunk, 0)
    lane = lax.broadcasted_iota(jnp.int32, (TILE, KV_COLS), 1)
    factor = jnp.where(lane < HEAD_SIZE, scale, 1.0)

    def finish(t, carry):
        dkv_ref[t] = (
            (acc_ref[t] * factor).astype(jnp.bfloat16).reshape(RING * CORES, PER_SEQ, KV_COLS)
        )
        return carry

    lax.fori_loop(0, LINE, finish, 0)


def input_kernel(place_ref, query_ref, rest_ref, own_ref, other_ref, out_ref):
    core = place_ref[1]
    query, rest = query_ref[...], rest_ref[...]
    part = RING // 2
    for y in range(LINE):
        for half in range(2):
            ring = slice(half * part, (half + 1) * part)
            own, other = own_ref[ring, y], other_ref[ring, y]
            weight = jnp.stack(
                [jnp.where(core == 0, own, other), jnp.where(core == 0, other, own)], axis=1
            ).reshape(part * CORES * WEIGHT_ROWS, -1)
            product = contract(query, weight[:, :Q_COLS], ((1,), (1,))) + contract(
                rest, weight[:, Q_COLS : Q_COLS + rest.shape[1]], ((1,), (1,))
            )
            width = product.shape[1]
            at = (2 * y + half) * width
            out_ref[:, at : at + width] = product.astype(jnp.bfloat16)


def term_kernel(terms_ref, a_ref, b_ref, held_ref):
    total = jnp.sum(terms_ref[...].astype(jnp.float32), axis=0) * TERM_SCALE
    a_ref[...] = total[:WEIGHT_ROWS]
    held_ref[...] = jnp.zeros_like(held_ref)
    held_ref[:B_ROWS] = total[WEIGHT_ROWS:]
    turned = held_ref[...].T
    b_ref[:, :B_ROWS] = turned[:ADAPTER_RANK, :B_ROWS]
    b_ref[:, B_ROWS:] = turned[ADAPTER_RANK:, :B_ROWS]


VMEM = pl.BlockSpec(memory_space=pltpu.VMEM)
SMEM = pl.BlockSpec(memory_space=pltpu.SMEM)
PARAMS = pltpu.CompilerParams(vmem_limit_bytes=48 * 2**20)


def attend(place, own, other, pairs):
    return pl.pallas_call(
        attention_kernel,
        out_shape=(
            jax.ShapeDtypeStruct((LINE, CORES, PER_SEQ, GROUP_WIDTH), jnp.bfloat16),
            jax.ShapeDtypeStruct((LINE, RING * CORES, PER_SEQ, KV_COLS), jnp.bfloat16),
        ),
        in_specs=[SMEM] + [VMEM] * 3,
        out_specs=(VMEM, VMEM),
        scratch_shapes=[
            pltpu.VMEM((LINE, TILE, KV_COLS), jnp.float32),
            pltpu.VMEM((LINE, KV_COLS, TILE), jnp.bfloat16),
            pltpu.VMEM((LINE, RING, CORES, WEIGHT_ROWS, GROUP_WIDTH), jnp.bfloat16),
        ],
        compiler_params=PARAMS,
        name="attention",
    )(place, own, other, pairs)


def term_sums(terms):
    return pl.pallas_call(
        term_kernel,
        out_shape=(
            jax.ShapeDtypeStruct((WEIGHT_ROWS, 2 * ADAPTER_RANK), jnp.float32),
            jax.ShapeDtypeStruct((ADAPTER_RANK, 2 * B_ROWS), jnp.float32),
        ),
        in_specs=[VMEM],
        out_specs=(VMEM, VMEM),
        scratch_shapes=[pltpu.VMEM((2 * ADAPTER_RANK, 2 * ADAPTER_RANK), jnp.float32)],
        compiler_params=PARAMS,
        name="term_sums",
    )(terms)


def input_product(place, query, rest, own, other):
    return pl.pallas_call(
        input_kernel,
        out_shape=jax.ShapeDtypeStruct((query.shape[0], MODEL_WIDTH), jnp.bfloat16),
        in_specs=[SMEM] + [VMEM] * 4,
        out_specs=VMEM,
        compiler_params=PARAMS,
        name="input_gradient",
    )(place, query, rest, own, other)


def exchange(blocks, axes):
    return lax.all_to_all(blocks, axes, split_axis=0, concat_axis=0, tiled=True)


def swap(block):
    return lax.ppermute(block, "core", [(0, 1), (1, 0)])


def from_next(block):
    sections = lax.axis_size("section")
    return lax.ppermute(block, "section", [((i + 1) % sections, i) for i in range(sections)])


def along(block, distance):
    return lax.ppermute(block, "y", [(y, (y + distance) % LINE) for y in range(LINE)])


def by_source(pieces, line_at):
    doubled = jnp.stack(pieces[::-1] + pieces[:0:-1])
    return lax.dynamic_slice_in_dim(doubled, LINE - 1 - line_at, LINE, 0)


def core_order(own, other, core, axis):
    return jnp.stack(
        [jnp.where(core == 0, own, other), jnp.where(core == 0, other, own)], axis=axis
    )


def ordered(first, second):
    return lax.optimization_barrier((first, second))


def per_device(
    hidden,
    queries,
    keys_values,
    out_grad,
    qkv_weight,
    out_weight,
    adapter_down_maps,
    adapter_up_maps,
):
    line_at = lax.axis_index("y")
    core = lax.axis_index("core")
    place = jnp.stack([lax.axis_index("z"), core]).astype(jnp.int32)
    tokens = SEQS * PER_SEQ
    halves = LINE // SEQS
    qkv_cols = WEIGHT_COLS - 2 * ADAPTER_RANK

    kv_part = keys_values[0].reshape(SEQS, PER_SEQ, halves, CORES, KV_COLS).transpose(0, 2, 3, 1, 4)
    out_part = (
        out_weight[0]
        .reshape(WEIGHT_ROWS, halves, CORES, 2, GROUP_WIDTH // 2)
        .transpose(1, 2, 3, 0, 4)
        .reshape(1, halves, CORES, 2 * WEIGHT_ROWS, GROUP_WIDTH // 2)
    )
    group_send = jnp.concatenate(
        [kv_part, jnp.broadcast_to(out_part, (SEQS,) + out_part.shape[1:])], axis=3
    ).reshape(LINE * CORES, PER_SEQ + 2 * WEIGHT_ROWS, KV_COLS)
    group_line = exchange(group_send, ("y", "core"))

    grad_part = jnp.broadcast_to(out_grad[0][:, None], (SEQS, halves, PER_SEQ, MODEL_WIDTH))
    query_part = queries[0].reshape(SEQS, PER_SEQ, halves, PAIR_WIDTH).transpose(0, 2, 1, 3)
    weights = jnp.concatenate([qkv_weight[0], adapter_down_maps[0]], axis=1)
    folded = jnp.concatenate([weights[:, :FOLD], weights[:, WEIGHT_COLS - FOLD :]], axis=0)
    weight_part = jnp.broadcast_to(folded, (SEQS, halves, PER_SEQ, FOLD))
    row_send = jnp.concatenate([grad_part, query_part, weight_part], axis=3).reshape(
        LINE, PER_SEQ, ROW_COLS + FOLD
    )
    group_line, row_send = ordered(group_line, row_send)
    group_all = lax.all_gather(group_line, "z", axis=0).reshape(
        RING, LINE, CORES, PER_SEQ + 2 * WEIGHT_ROWS, KV_COLS
    )
    row_own = exchange(row_send, ("y",))
    row_other = swap(row_own)
    weight_line = jnp.concatenate(
        [
            row_own[:, :WEIGHT_ROWS, ROW_COLS:],
            row_own[:, WEIGHT_ROWS:, ROW_COLS + 2 * FOLD - WEIGHT_COLS :],
        ],
        axis=2,
    )
    group_all, weight_line = ordered(group_all, weight_line)
    weight_own = lax.all_gather(weight_line, "z", axis=0)

    query_gradient, kv_grad = attend(place, row_own, row_other, group_all)
    kv_back = exchange(kv_grad.reshape(DEVICES, PER_SEQ, KV_COLS), SEQ_AXES)

    query_chip = core_order(query_gradient[:, 0], swap(query_gradient[:, 1]), core, 1)
    query_sends = [
        lax.dynamic_index_in_dim(query_chip, (line_at + d) % LINE, 0, keepdims=False)
        for d in range(LINE)
    ]
    query_sends[0], weight_own = ordered(query_sends[0], weight_own)
    weight_other = swap(weight_own)
    query_back = by_source(
        query_sends[:1] + [along(query_sends[d], d) for d in range(1, LINE)], line_at
    )
    query_local = (
        query_back.reshape(SEQS, halves * CORES, PER_SEQ, GROUP_WIDTH)
        .transpose(0, 2, 1, 3)
        .reshape(tokens, Q_COLS)
    )
    kv_local = (
        jnp.sum(
            kv_back.reshape(SEQS, halves, RING, CORES, PER_SEQ, KV_COLS).astype(jnp.float32), axis=2
        )
        .astype(jnp.bfloat16)
        .reshape(SEQS, KEY_VALUE_HEADS, PER_SEQ, 2, HEAD_SIZE)
        .transpose(0, 2, 3, 1, 4)
        .reshape(tokens, 2 * KEY_VALUE_HEADS * HEAD_SIZE)
    )
    value_local = kv_local[:, KEY_VALUE_HEADS * HEAD_SIZE :]
    up_maps = adapter_up_maps[0]
    adapter_between = jnp.concatenate(
        [
            contract(query_local, up_maps[:, :Q_COLS], ((1,), (1,))),
            contract(value_local, up_maps[:, Q_COLS:], ((1,), (1,))),
        ],
        axis=1,
    ).astype(jnp.bfloat16)
    down_own, down_other = weight_own[..., qkv_cols:], weight_other[..., qkv_cols:]
    down_all = (
        core_order(down_own, down_other, core, 2)
        .transpose(1, 0, 2, 3, 4)
        .reshape(MODEL_WIDTH, 2 * ADAPTER_RANK)
    )

    hidden_rows = hidden[0].reshape(tokens, MODEL_WIDTH)
    adapter_reduced = dot(hidden_rows, down_all).astype(jnp.bfloat16)
    a_term = contract(hidden_rows, adapter_between, ((0,), (0,)))
    b_turned = jnp.concatenate(
        [
            contract(query_local, adapter_reduced[:, :ADAPTER_RANK], ((0,), (0,))),
            contract(value_local, adapter_reduced[:, ADAPTER_RANK:], ((0,), (0,))),
        ],
        axis=0,
    )
    ranks = 2 * ADAPTER_RANK
    a_send = a_term.reshape(LINE * RING, CORES, WEIGHT_ROWS, ranks)
    b_send = b_turned.reshape(LINE * RING, CORES, 2, B_ROWS, ADAPTER_RANK)
    b_send = jnp.concatenate([b_send[:, :, 0], b_send[:, :, 1]], axis=3)
    term_send = jnp.concatenate([a_send, b_send], axis=2)
    kept = lax.dynamic_index_in_dim(term_send, core, 1, keepdims=False)
    given = lax.dynamic_index_in_dim(term_send, 1 - core, 1, keepdims=False)
    term_chip = (kept + swap(given)).astype(jnp.bfloat16)
    a_sum, b_sum = term_sums(exchange(term_chip, ("y", "z")))

    rest = jnp.concatenate([kv_local, adapter_between * jnp.bfloat16(ADAPTER_SCALE)], axis=1)
    input_gradient = input_product(place, query_local, rest, weight_own, weight_other)
    passed = from_next(input_gradient.reshape(1, SEQS, PER_SEQ, MODEL_WIDTH))
    return (passed, a_sum[None], b_sum[None])


def solution(mesh):
    sections = mesh.shape["section"]
    fine = Mesh(mesh.devices.reshape(sections, LINE, RING, CORES), ("section",) + SEQ_AXES)
    return jax.shard_map(
        per_device,
        mesh=fine,
        in_specs=(
            P("section", None, SEQ_AXES, None),
            P("section", None, SEQ_AXES, None),
            P("section", None, SEQ_AXES, None),
            P("section", None, SEQ_AXES, None),
            P("section", SEQ_AXES, None),
            P("section", SEQ_AXES, None),
            P("section", SEQ_AXES, None),
            P("section", None, None),
        ),
        out_specs=(
            P("section", None, SEQ_AXES, None),
            P("section", SEQ_AXES, None),
            P("section", None, SEQ_AXES),
        ),
        check_vma=False,
    )
```

```python
import jax
import jax.numpy as jnp
from jax import lax
from jax.experimental import pallas as pl
from jax.experimental.pallas import tpu as pltpu
from jax.sharding import Mesh, PartitionSpec as P

MODEL_WIDTH = 2048
QUERY_HEADS = 16
KEY_VALUE_HEADS = 4
HEAD_SIZE = 64
ADAPTER_RANK = 64
ADAPTER_NUMER = 128
GRADIENT_SCALE = 32
SEQS = 2
LEN = 4096

LINE = 4
RING = 8
CORES = 2
SEQ_AXES = ("y", "z", "core")
DEVICES = LINE * RING * CORES
PER_SEQ = LEN // DEVICES
Q_COLS = QUERY_HEADS * HEAD_SIZE
KV_COLS = 2 * HEAD_SIZE
GROUP = QUERY_HEADS // KEY_VALUE_HEADS
GROUP_WIDTH = GROUP * HEAD_SIZE
PAIR_WIDTH = CORES * GROUP_WIDTH
WEIGHT_ROWS = MODEL_WIDTH // DEVICES
B_ROWS = (QUERY_HEADS + KEY_VALUE_HEADS) * HEAD_SIZE // DEVICES // 2
ADAPTER_SCALE = ADAPTER_NUMER / ADAPTER_RANK
TERM_SCALE = ADAPTER_SCALE / GRADIENT_SCALE
ROW_COLS = MODEL_WIDTH + PAIR_WIDTH
WEIGHT_COLS = Q_COLS + 2 * KEY_VALUE_HEADS * HEAD_SIZE + 2 * ADAPTER_RANK
FOLD = 896

CHUNK = CORES * PER_SEQ
SPAN = RING * CHUNK
COLS = GROUP * CHUNK
TILE = SPAN
EXP_SCALE = HEAD_SIZE ** (-0.5) * 1.4426950408889634


def dot(a, b):
    return jnp.dot(a, b, preferred_element_type=jnp.float32)


def contract(a, b, dims):
    return lax.dot_general(a, b, (dims, ((), ())), preferred_element_type=jnp.float32)


def head_columns(rows):
    turned = rows.astype(jnp.float32).T
    return jnp.concatenate(
        [turned[h * HEAD_SIZE : (h + 1) * HEAD_SIZE] for h in range(GROUP)], axis=1
    )


def causal_mask(part, core):
    key_pos = lax.broadcasted_iota(jnp.int32, (TILE, COLS), 0)
    row = lax.broadcasted_iota(jnp.int32, (TILE, COLS), 1) % CHUNK
    row_pos = part * CHUNK + (row + core * PER_SEQ) % CHUNK
    return row_pos >= key_pos


def tile_of(pair_ref, t):
    return pair_ref[:, t, :, :PER_SEQ, :].reshape(TILE, KV_COLS)


def query_rows_of(own_ref, other_ref, j, core):
    columns = pl.ds(pl.multiple_of(MODEL_WIDTH + core * GROUP_WIDTH, GROUP_WIDTH), GROUP_WIDTH)
    return jnp.concatenate([own_ref[j, :, columns], other_ref[j, :, columns]], axis=0)


def attention_kernel(
    place_ref, own_ref, other_ref, pair_ref, dq_ref, dkv_ref, acc_ref, turned_ref, weight_ref
):
    part, core = place_ref[0], place_ref[1]
    scale = HEAD_SIZE ** (-0.5)
    acc_ref[...] = jnp.zeros_like(acc_ref)

    def prepare(t, carry):
        turned_ref[t] = tile_of(pair_ref, t).T
        for z in range(RING):
            for c in range(CORES):
                block = pair_ref[z, t, c, PER_SEQ:, :]
                weight_ref[t, z, c] = jnp.concatenate(
                    [block[:WEIGHT_ROWS], block[WEIGHT_ROWS:]], axis=1
                )
        return carry

    lax.fori_loop(0, LINE, prepare, 0)
    weight = weight_ref[...].reshape(MODEL_WIDTH, GROUP_WIDTH)

    def chunk(j, carry):
        query_half = head_columns(query_rows_of(own_ref, other_ref, j, core))
        out_grad = jnp.concatenate(
            [own_ref[j, :, :MODEL_WIDTH], other_ref[j, :, :MODEL_WIDTH]], axis=0
        )
        grad_half = head_columns(dot(out_grad, weight).astype(jnp.bfloat16))
        blank = jnp.zeros_like(query_half)
        query_full = jnp.concatenate([query_half, blank], axis=0)
        grad_full = jnp.concatenate([blank, grad_half], axis=0)
        query_cols = query_full.astype(jnp.bfloat16)
        grad_cols = grad_full.astype(jnp.bfloat16)
        query_rows = query_full.T.astype(jnp.bfloat16)
        grad_rows = grad_full.T.astype(jnp.bfloat16)

        def scores_of(t, masked):
            scores = dot(tile_of(pair_ref, t), query_cols)
            if masked:
                scores = jnp.where(causal_mask(part, core), scores, -jnp.inf)
            return scores

        def forward_tile(t, state, masked):
            top, total, mixed = state
            scores = scores_of(t, masked)
            new_top = jnp.maximum(top, jnp.max(scores, axis=0, keepdims=True))
            shrink = jnp.exp2((top - new_top) * EXP_SCALE)
            power = jnp.exp2(scores * EXP_SCALE - new_top * EXP_SCALE)
            total = total * shrink + jnp.sum(power, axis=0, keepdims=True)
            mixed = mixed * shrink + dot(turned_ref[t, HEAD_SIZE:], power.astype(jnp.bfloat16))
            return new_top, total, mixed

        state = (
            jnp.full((1, COLS), -jnp.inf, jnp.float32),
            jnp.zeros((1, COLS), jnp.float32),
            jnp.zeros((HEAD_SIZE, COLS), jnp.float32),
        )
        state = lax.fori_loop(0, j, lambda t, s: forward_tile(t, s, False), state)
        top, total, mixed = forward_tile(j, state, True)
        delta = jnp.sum(grad_half * (mixed / total), axis=0, keepdims=True)
        log_total = top * EXP_SCALE + jnp.log2(total)

        def backward_tile(t, query_sum, masked):
            prob = jnp.exp2(scores_of(t, masked) * EXP_SCALE - log_total)
            prob_grad = dot(tile_of(pair_ref, t), grad_cols)
            score_grad = (prob * (prob_grad - delta)).astype(jnp.bfloat16)
            acc_ref[t] += dot(score_grad, query_rows) + dot(prob.astype(jnp.bfloat16), grad_rows)
            return query_sum + dot(turned_ref[t, :HEAD_SIZE], score_grad)

        query_sum = lax.fori_loop(
            0,
            j,
            lambda t, s: backward_tile(t, s, False),
            jnp.zeros((HEAD_SIZE, COLS), jnp.float32),
        )
        query_sum = backward_tile(j, query_sum, True) * scale
        stacked = jnp.concatenate(
            [query_sum[:, h * CHUNK : (h + 1) * CHUNK] for h in range(GROUP)], axis=0
        )
        dq_ref[j] = stacked.T.astype(jnp.bfloat16).reshape(CORES, PER_SEQ, GROUP_WIDTH)
        return carry

    lax.fori_loop(0, LINE, chunk, 0)
    lane = lax.broadcasted_iota(jnp.int32, (TILE, KV_COLS), 1)
    factor = jnp.where(lane < HEAD_SIZE, scale, 1.0)

    def finish(t, carry):
        dkv_ref[t] = (
            (acc_ref[t] * factor).astype(jnp.bfloat16).reshape(RING * CORES, PER_SEQ, KV_COLS)
        )
        return carry

    lax.fori_loop(0, LINE, finish, 0)


def token_kernel(query_ref, kv_ref, query_up_ref, value_up_ref, pairs_ref, between_ref):
    halves = LINE // SEQS
    rows = []
    for s in range(SEQS):
        groups = []
        for g in range(KEY_VALUE_HEADS):
            first = ((s * halves + g // CORES) * RING) * CORES + g % CORES
            total = kv_ref[first].astype(jnp.float32)
            for z in range(1, RING):
                total = total + kv_ref[first + z * CORES].astype(jnp.float32)
            groups.append(total)
        rows.append(jnp.concatenate(groups, axis=1))
    pairs = jnp.concatenate(rows, axis=0).astype(jnp.bfloat16)
    pairs_ref[...] = pairs
    between_ref[...] = (
        contract(query_ref[...], query_up_ref[...], ((1,), (1,)))
        + contract(pairs, value_up_ref[...], ((1,), (1,)))
    ).astype(jnp.bfloat16)


def input_kernel(place_ref, query_ref, pairs_ref, between_ref, own_ref, other_ref, out_ref):
    core = place_ref[1]
    query, pairs = query_ref[...], pairs_ref[...]
    scaled = between_ref[...] * jnp.bfloat16(ADAPTER_SCALE)
    kv_end = WEIGHT_COLS - 2 * ADAPTER_RANK
    part = RING // 2
    for y in range(LINE):
        for half in range(2):
            ring = slice(half * part, (half + 1) * part)
            own, other = own_ref[ring, y], other_ref[ring, y]
            weight = jnp.stack(
                [jnp.where(core == 0, own, other), jnp.where(core == 0, other, own)], axis=1
            ).reshape(part * CORES * WEIGHT_ROWS, WEIGHT_COLS)
            product = (
                contract(query, weight[:, :Q_COLS], ((1,), (1,)))
                + contract(pairs, weight[:, Q_COLS:kv_end], ((1,), (1,)))
                + contract(scaled, weight[:, kv_end:], ((1,), (1,)))
            )
            width = product.shape[1]
            at = (2 * y + half) * width
            out_ref[:, at : at + width] = product.astype(jnp.bfloat16)


def term_kernel(terms_ref, a_ref, b_ref, held_ref):
    total = jnp.sum(terms_ref[...].astype(jnp.float32), axis=0) * TERM_SCALE
    a_ref[...] = total[:WEIGHT_ROWS]
    held_ref[...] = jnp.zeros_like(held_ref)
    held_ref[:B_ROWS] = total[WEIGHT_ROWS:]
    turned = held_ref[...].T
    b_ref[:, :B_ROWS] = turned[:ADAPTER_RANK, :B_ROWS]
    b_ref[:, B_ROWS:] = turned[ADAPTER_RANK:, :B_ROWS]


VMEM = pl.BlockSpec(memory_space=pltpu.VMEM)
SMEM = pl.BlockSpec(memory_space=pltpu.SMEM)
PARAMS = pltpu.CompilerParams(vmem_limit_bytes=48 * 2**20)


def attend(place, own, other, pairs):
    return pl.pallas_call(
        attention_kernel,
        out_shape=(
            jax.ShapeDtypeStruct((LINE, CORES, PER_SEQ, GROUP_WIDTH), jnp.bfloat16),
            jax.ShapeDtypeStruct((LINE, RING * CORES, PER_SEQ, KV_COLS), jnp.bfloat16),
        ),
        in_specs=[SMEM] + [VMEM] * 3,
        out_specs=(VMEM, VMEM),
        scratch_shapes=[
            pltpu.VMEM((LINE, TILE, KV_COLS), jnp.float32),
            pltpu.VMEM((LINE, KV_COLS, TILE), jnp.bfloat16),
            pltpu.VMEM((LINE, RING, CORES, WEIGHT_ROWS, GROUP_WIDTH), jnp.bfloat16),
        ],
        compiler_params=PARAMS,
        name="attention",
    )(place, own, other, pairs)


def term_sums(terms):
    return pl.pallas_call(
        term_kernel,
        out_shape=(
            jax.ShapeDtypeStruct((WEIGHT_ROWS, 2 * ADAPTER_RANK), jnp.float32),
            jax.ShapeDtypeStruct((ADAPTER_RANK, 2 * B_ROWS), jnp.float32),
        ),
        in_specs=[VMEM],
        out_specs=(VMEM, VMEM),
        scratch_shapes=[pltpu.VMEM((2 * ADAPTER_RANK, 2 * ADAPTER_RANK), jnp.float32)],
        compiler_params=PARAMS,
        name="term_sums",
    )(terms)


def token_gradients(query, kv_back, query_up, value_up):
    tokens = query.shape[0]
    return pl.pallas_call(
        token_kernel,
        out_shape=(
            jax.ShapeDtypeStruct((tokens, KEY_VALUE_HEADS * KV_COLS), jnp.bfloat16),
            jax.ShapeDtypeStruct((tokens, 2 * ADAPTER_RANK), jnp.bfloat16),
        ),
        in_specs=[VMEM] * 4,
        out_specs=(VMEM, VMEM),
        compiler_params=PARAMS,
        cost_estimate=pl.CostEstimate(
            flops=16 * 10**9, bytes_accessed=2 * 2**20, transcendentals=0
        ),
        name="token_gradients",
    )(query, kv_back, query_up, value_up)


def input_product(place, query, pairs, between, own, other):
    return pl.pallas_call(
        input_kernel,
        out_shape=jax.ShapeDtypeStruct((query.shape[0], MODEL_WIDTH), jnp.bfloat16),
        in_specs=[SMEM] + [VMEM] * 5,
        out_specs=VMEM,
        compiler_params=PARAMS,
        name="input_gradient",
    )(place, query, pairs, between, own, other)


def exchange(blocks, axes):
    return lax.all_to_all(blocks, axes, split_axis=0, concat_axis=0, tiled=True)


def swap(block):
    return lax.ppermute(block, "core", [(0, 1), (1, 0)])


def from_next(block):
    sections = lax.axis_size("section")
    return lax.ppermute(block, "section", [((i + 1) % sections, i) for i in range(sections)])


def along(block, distance):
    return lax.ppermute(block, "y", [(y, (y + distance) % LINE) for y in range(LINE)])


def by_source(pieces, line_at):
    doubled = jnp.stack(pieces[::-1] + pieces[:0:-1])
    return lax.dynamic_slice_in_dim(doubled, LINE - 1 - line_at, LINE, 0)


def core_order(own, other, core, axis):
    return jnp.stack(
        [jnp.where(core == 0, own, other), jnp.where(core == 0, other, own)], axis=axis
    )


def ordered(first, second):
    return lax.optimization_barrier((first, second))


def per_device(
    hidden,
    queries,
    keys_values,
    out_grad,
    qkv_weight,
    out_weight,
    adapter_down_maps,
    adapter_up_maps,
):
    line_at = lax.axis_index("y")
    core = lax.axis_index("core")
    place = jnp.stack([lax.axis_index("z"), core]).astype(jnp.int32)
    tokens = SEQS * PER_SEQ
    halves = LINE // SEQS
    qkv_cols = WEIGHT_COLS - 2 * ADAPTER_RANK

    kv_part = keys_values[0].reshape(SEQS, PER_SEQ, halves, CORES, KV_COLS).transpose(0, 2, 3, 1, 4)
    out_part = (
        out_weight[0]
        .reshape(WEIGHT_ROWS, halves, CORES, 2, GROUP_WIDTH // 2)
        .transpose(1, 2, 3, 0, 4)
        .reshape(1, halves, CORES, 2 * WEIGHT_ROWS, GROUP_WIDTH // 2)
    )
    group_send = jnp.concatenate(
        [kv_part, jnp.broadcast_to(out_part, (SEQS,) + out_part.shape[1:])], axis=3
    ).reshape(LINE * CORES, PER_SEQ + 2 * WEIGHT_ROWS, KV_COLS)
    group_line = exchange(group_send, ("y", "core"))

    grad_part = jnp.broadcast_to(out_grad[0][:, None], (SEQS, halves, PER_SEQ, MODEL_WIDTH))
    query_part = queries[0].reshape(SEQS, PER_SEQ, halves, PAIR_WIDTH).transpose(0, 2, 1, 3)
    kv_weight = (
        qkv_weight[0, :, Q_COLS:]
        .reshape(WEIGHT_ROWS, 2, KEY_VALUE_HEADS, HEAD_SIZE)
        .transpose(0, 2, 1, 3)
        .reshape(WEIGHT_ROWS, KEY_VALUE_HEADS * KV_COLS)
    )
    weights = jnp.concatenate(
        [qkv_weight[0, :, :Q_COLS], kv_weight, adapter_down_maps[0]], axis=1
    )
    folded = jnp.concatenate([weights[:, :FOLD], weights[:, WEIGHT_COLS - FOLD :]], axis=0)
    weight_part = jnp.broadcast_to(folded, (SEQS, halves, PER_SEQ, FOLD))
    row_send = jnp.concatenate([grad_part, query_part, weight_part], axis=3).reshape(
        LINE, PER_SEQ, ROW_COLS + FOLD
    )
    group_line, row_send = ordered(group_line, row_send)
    group_all = lax.all_gather(group_line, "z", axis=0).reshape(
        RING, LINE, CORES, PER_SEQ + 2 * WEIGHT_ROWS, KV_COLS
    )
    row_own = exchange(row_send, ("y",))
    row_other = swap(row_own)
    weight_line = jnp.concatenate(
        [
            row_own[:, :WEIGHT_ROWS, ROW_COLS:],
            row_own[:, WEIGHT_ROWS:, ROW_COLS + 2 * FOLD - WEIGHT_COLS :],
        ],
        axis=2,
    )
    group_all, weight_line = ordered(group_all, weight_line)
    weight_own = lax.all_gather(weight_line, "z", axis=0)

    query_gradient, kv_grad = attend(place, row_own, row_other, group_all)
    kv_back = exchange(kv_grad.reshape(DEVICES, PER_SEQ, KV_COLS), SEQ_AXES)

    query_chip = core_order(query_gradient[:, 0], swap(query_gradient[:, 1]), core, 1)
    query_sends = [
        lax.dynamic_index_in_dim(query_chip, (line_at + d) % LINE, 0, keepdims=False)
        for d in range(LINE)
    ]
    query_sends[0], weight_own = ordered(query_sends[0], weight_own)
    weight_other = swap(weight_own)
    query_back = by_source(
        query_sends[:1] + [along(query_sends[d], d) for d in range(1, LINE)], line_at
    )
    query_local = (
        query_back.reshape(SEQS, halves * CORES, PER_SEQ, GROUP_WIDTH)
        .transpose(0, 2, 1, 3)
        .reshape(tokens, Q_COLS)
    )
    up_maps = adapter_up_maps[0]
    query_up = jnp.pad(up_maps[:, :Q_COLS], ((0, ADAPTER_RANK), (0, 0)))
    value_up = jnp.pad(
        up_maps[:, Q_COLS:].reshape(ADAPTER_RANK, KEY_VALUE_HEADS, 1, HEAD_SIZE),
        ((ADAPTER_RANK, 0), (0, 0), (1, 0), (0, 0)),
    ).reshape(2 * ADAPTER_RANK, KEY_VALUE_HEADS * KV_COLS)
    kv_local, adapter_between = token_gradients(query_local, kv_back, query_up, value_up)
    input_gradient = input_product(
        place, query_local, kv_local, adapter_between, weight_own, weight_other
    )
    passed = from_next(input_gradient.reshape(1, SEQS, PER_SEQ, MODEL_WIDTH))

    down_own, down_other = weight_own[..., qkv_cols:], weight_other[..., qkv_cols:]
    down_all = (
        core_order(down_own, down_other, core, 2)
        .transpose(1, 0, 2, 3, 4)
        .reshape(MODEL_WIDTH, 2 * ADAPTER_RANK)
    )

    hidden_rows = hidden[0].reshape(tokens, MODEL_WIDTH)
    adapter_reduced = dot(hidden_rows, down_all).astype(jnp.bfloat16)
    a_term = contract(hidden_rows, adapter_between, ((0,), (0,)))
    value_term = contract(kv_local, adapter_reduced[:, ADAPTER_RANK:], ((0,), (0,)))
    value_term = value_term.reshape(KEY_VALUE_HEADS, 2, HEAD_SIZE, ADAPTER_RANK)[:, 1]
    b_turned = jnp.concatenate(
        [
            contract(query_local, adapter_reduced[:, :ADAPTER_RANK], ((0,), (0,))),
            value_term.reshape(KEY_VALUE_HEADS * HEAD_SIZE, ADAPTER_RANK),
        ],
        axis=0,
    )
    a_send = a_term.astype(jnp.bfloat16).reshape(DEVICES, WEIGHT_ROWS, 2 * ADAPTER_RANK)
    b_send = b_turned.astype(jnp.bfloat16).reshape(DEVICES, 2, B_ROWS, ADAPTER_RANK)
    b_send = jnp.concatenate([b_send[:, 0], b_send[:, 1]], axis=2)
    term_send = jnp.concatenate([a_send, b_send], axis=1)
    a_sum, b_sum = term_sums(exchange(term_send, SEQ_AXES))

    return (passed, a_sum[None], b_sum[None])


def solution(mesh):
    sections = mesh.shape["section"]
    fine = Mesh(mesh.devices.reshape(sections, LINE, RING, CORES), ("section",) + SEQ_AXES)
    return jax.shard_map(
        per_device,
        mesh=fine,
        in_specs=(
            P("section", None, SEQ_AXES, None),
            P("section", None, SEQ_AXES, None),
            P("section", None, SEQ_AXES, None),
            P("section", None, SEQ_AXES, None),
            P("section", SEQ_AXES, None),
            P("section", SEQ_AXES, None),
            P("section", SEQ_AXES, None),
            P("section", None, None),
        ),
        out_specs=(
            P("section", None, SEQ_AXES, None),
            P("section", SEQ_AXES, None),
            P("section", None, SEQ_AXES),
        ),
        check_vma=False,
    )
```

```python
import jax
import jax.numpy as jnp
from jax import lax
from jax.experimental import pallas as pl
from jax.experimental.pallas import tpu as pltpu
from jax.sharding import Mesh, PartitionSpec as P

MODEL_WIDTH = 2048
QUERY_HEADS = 16
KEY_VALUE_HEADS = 4
HEAD_SIZE = 64
ADAPTER_RANK = 64
ADAPTER_NUMER = 128
GRADIENT_SCALE = 32
SEQS = 2
LEN = 4096

LINE = 4
RING = 8
CORES = 2
SEQ_AXES = ("y", "z", "core")
DEVICES = LINE * RING * CORES
PER_SEQ = LEN // DEVICES
Q_COLS = QUERY_HEADS * HEAD_SIZE
KV_COLS = 2 * HEAD_SIZE
GROUP = QUERY_HEADS // KEY_VALUE_HEADS
GROUP_WIDTH = GROUP * HEAD_SIZE
PAIR_WIDTH = CORES * GROUP_WIDTH
WEIGHT_ROWS = MODEL_WIDTH // DEVICES
B_ROWS = (QUERY_HEADS + KEY_VALUE_HEADS) * HEAD_SIZE // DEVICES // 2
ADAPTER_SCALE = ADAPTER_NUMER / ADAPTER_RANK
TERM_SCALE = ADAPTER_SCALE / GRADIENT_SCALE
ROW_COLS = MODEL_WIDTH + PAIR_WIDTH
WEIGHT_COLS = Q_COLS + 2 * KEY_VALUE_HEADS * HEAD_SIZE + 2 * ADAPTER_RANK
FOLD = 896

CHUNK = CORES * PER_SEQ
SPAN = RING * CHUNK
COLS = GROUP * CHUNK
TILE = SPAN
EXP_SCALE = HEAD_SIZE ** (-0.5) * 1.4426950408889634


def dot(a, b):
    return jnp.dot(a, b, preferred_element_type=jnp.float32)


def contract(a, b, dims):
    return lax.dot_general(a, b, (dims, ((), ())), preferred_element_type=jnp.float32)


def head_columns(rows):
    turned = rows.astype(jnp.float32).T
    return jnp.concatenate(
        [turned[h * HEAD_SIZE : (h + 1) * HEAD_SIZE] for h in range(GROUP)], axis=1
    )


def causal_mask(part, core):
    key_pos = lax.broadcasted_iota(jnp.int32, (TILE, COLS), 0)
    row = lax.broadcasted_iota(jnp.int32, (TILE, COLS), 1) % CHUNK
    row_pos = part * CHUNK + (row + core * PER_SEQ) % CHUNK
    return row_pos >= key_pos


def tile_of(pair_ref, t):
    return pair_ref[:, t, :, :PER_SEQ, :].reshape(TILE, KV_COLS)


def query_rows_of(own_ref, other_ref, j, core):
    columns = pl.ds(pl.multiple_of(MODEL_WIDTH + core * GROUP_WIDTH, GROUP_WIDTH), GROUP_WIDTH)
    return jnp.concatenate([own_ref[j, :, columns], other_ref[j, :, columns]], axis=0)


def attention_kernel(
    place_ref, own_ref, other_ref, pair_ref, dq_ref, dkv_ref, acc_ref, turned_ref, weight_ref
):
    part, core = place_ref[0], place_ref[1]
    scale = HEAD_SIZE ** (-0.5)
    acc_ref[...] = jnp.zeros_like(acc_ref)

    def prepare(t, carry):
        turned_ref[t] = tile_of(pair_ref, t).T
        for z in range(RING):
            for c in range(CORES):
                block = pair_ref[z, t, c, PER_SEQ:, :]
                weight_ref[t, z, c] = jnp.concatenate(
                    [block[:WEIGHT_ROWS], block[WEIGHT_ROWS:]], axis=1
                )
        return carry

    lax.fori_loop(0, LINE, prepare, 0)
    weight = weight_ref[...].reshape(MODEL_WIDTH, GROUP_WIDTH)

    def chunk(j, carry):
        query_half = head_columns(query_rows_of(own_ref, other_ref, j, core))
        out_grad = jnp.concatenate(
            [own_ref[j, :, :MODEL_WIDTH], other_ref[j, :, :MODEL_WIDTH]], axis=0
        )
        grad_half = head_columns(dot(out_grad, weight).astype(jnp.bfloat16))
        blank = jnp.zeros_like(query_half)
        query_full = jnp.concatenate([query_half, blank], axis=0)
        grad_full = jnp.concatenate([blank, grad_half], axis=0)
        query_cols = query_full.astype(jnp.bfloat16)
        grad_cols = grad_full.astype(jnp.bfloat16)
        query_rows = query_full.T.astype(jnp.bfloat16)
        grad_rows = grad_full.T.astype(jnp.bfloat16)

        def scores_of(t, masked):
            scores = dot(tile_of(pair_ref, t), query_cols)
            if masked:
                scores = jnp.where(causal_mask(part, core), scores, -jnp.inf)
            return scores

        def forward_tile(t, state, masked):
            top, total, mixed = state
            scores = scores_of(t, masked)
            new_top = jnp.maximum(top, jnp.max(scores, axis=0, keepdims=True))
            shrink = jnp.exp2((top - new_top) * EXP_SCALE)
            power = jnp.exp2(scores * EXP_SCALE - new_top * EXP_SCALE)
            total = total * shrink + jnp.sum(power, axis=0, keepdims=True)
            mixed = mixed * shrink + dot(turned_ref[t, HEAD_SIZE:], power.astype(jnp.bfloat16))
            return new_top, total, mixed

        state = (
            jnp.full((1, COLS), -jnp.inf, jnp.float32),
            jnp.zeros((1, COLS), jnp.float32),
            jnp.zeros((HEAD_SIZE, COLS), jnp.float32),
        )
        state = lax.fori_loop(0, j, lambda t, s: forward_tile(t, s, False), state)
        top, total, mixed = forward_tile(j, state, True)
        delta = jnp.sum(grad_half * (mixed / total), axis=0, keepdims=True)
        log_total = top * EXP_SCALE + jnp.log2(total)

        def backward_tile(t, query_sum, masked):
            prob = jnp.exp2(scores_of(t, masked) * EXP_SCALE - log_total)
            prob_grad = dot(tile_of(pair_ref, t), grad_cols)
            score_grad = (prob * (prob_grad - delta)).astype(jnp.bfloat16)
            acc_ref[t] += dot(score_grad, query_rows) + dot(prob.astype(jnp.bfloat16), grad_rows)
            return query_sum + dot(turned_ref[t, :HEAD_SIZE], score_grad)

        query_sum = lax.fori_loop(
            0,
            j,
            lambda t, s: backward_tile(t, s, False),
            jnp.zeros((HEAD_SIZE, COLS), jnp.float32),
        )
        query_sum = backward_tile(j, query_sum, True) * scale
        stacked = jnp.concatenate(
            [query_sum[:, h * CHUNK : (h + 1) * CHUNK] for h in range(GROUP)], axis=0
        )
        dq_ref[j] = stacked.T.astype(jnp.bfloat16).reshape(CORES, PER_SEQ, GROUP_WIDTH)
        return carry

    lax.fori_loop(0, LINE, chunk, 0)
    lane = lax.broadcasted_iota(jnp.int32, (TILE, KV_COLS), 1)
    factor = jnp.where(lane < HEAD_SIZE, scale, 1.0)

    def finish(t, carry):
        dkv_ref[t] = (
            (acc_ref[t] * factor).astype(jnp.bfloat16).reshape(RING * CORES, PER_SEQ, KV_COLS)
        )
        return carry

    lax.fori_loop(0, LINE, finish, 0)


def token_kernel(query_ref, kv_ref, query_up_ref, value_up_ref, pairs_ref, between_ref):
    halves = LINE // SEQS
    rows = []
    for s in range(SEQS):
        groups = []
        for g in range(KEY_VALUE_HEADS):
            first = ((s * halves + g // CORES) * RING) * CORES + g % CORES
            total = kv_ref[first].astype(jnp.float32)
            for z in range(1, RING):
                total = total + kv_ref[first + z * CORES].astype(jnp.float32)
            groups.append(total)
        rows.append(jnp.concatenate(groups, axis=1))
    pairs = jnp.concatenate(rows, axis=0).astype(jnp.bfloat16)
    pairs_ref[...] = pairs
    between_ref[...] = (
        contract(query_ref[...], query_up_ref[...], ((1,), (1,)))
        + contract(pairs, value_up_ref[...], ((1,), (1,)))
    ).astype(jnp.bfloat16)


def input_kernel(place_ref, query_ref, pairs_ref, between_ref, own_ref, other_ref, out_ref):
    core = place_ref[1]
    query, pairs = query_ref[...], pairs_ref[...]
    scaled = between_ref[...] * jnp.bfloat16(ADAPTER_SCALE)
    kv_end = WEIGHT_COLS - 2 * ADAPTER_RANK
    part = RING // 2
    for y in range(LINE):
        for half in range(2):
            ring = slice(half * part, (half + 1) * part)
            own, other = own_ref[ring, y], other_ref[ring, y]
            weight = jnp.stack(
                [jnp.where(core == 0, own, other), jnp.where(core == 0, other, own)], axis=1
            ).reshape(part * CORES * WEIGHT_ROWS, WEIGHT_COLS)
            product = (
                contract(query, weight[:, :Q_COLS], ((1,), (1,)))
                + contract(pairs, weight[:, Q_COLS:kv_end], ((1,), (1,)))
                + contract(scaled, weight[:, kv_end:], ((1,), (1,)))
            )
            width = product.shape[1]
            at = (2 * y + half) * width
            out_ref[:, at : at + width] = product.astype(jnp.bfloat16)


def term_kernel(terms_ref, a_ref, b_ref, held_ref):
    total = jnp.sum(terms_ref[...].astype(jnp.float32), axis=0) * TERM_SCALE
    a_ref[...] = total[:WEIGHT_ROWS]
    held_ref[...] = jnp.zeros_like(held_ref)
    held_ref[:B_ROWS] = total[WEIGHT_ROWS:]
    turned = held_ref[...].T
    b_ref[:, :B_ROWS] = turned[:ADAPTER_RANK, :B_ROWS]
    b_ref[:, B_ROWS:] = turned[ADAPTER_RANK:, :B_ROWS]


VMEM = pl.BlockSpec(memory_space=pltpu.VMEM)
SMEM = pl.BlockSpec(memory_space=pltpu.SMEM)
PARAMS = pltpu.CompilerParams(vmem_limit_bytes=48 * 2**20)


def attend(place, own, other, pairs):
    return pl.pallas_call(
        attention_kernel,
        out_shape=(
            jax.ShapeDtypeStruct((LINE, CORES, PER_SEQ, GROUP_WIDTH), jnp.bfloat16),
            jax.ShapeDtypeStruct((LINE, RING * CORES, PER_SEQ, KV_COLS), jnp.bfloat16),
        ),
        in_specs=[SMEM] + [VMEM] * 3,
        out_specs=(VMEM, VMEM),
        scratch_shapes=[
            pltpu.VMEM((LINE, TILE, KV_COLS), jnp.float32),
            pltpu.VMEM((LINE, KV_COLS, TILE), jnp.bfloat16),
            pltpu.VMEM((LINE, RING, CORES, WEIGHT_ROWS, GROUP_WIDTH), jnp.bfloat16),
        ],
        compiler_params=PARAMS,
        name="attention",
    )(place, own, other, pairs)


def term_sums(terms):
    return pl.pallas_call(
        term_kernel,
        out_shape=(
            jax.ShapeDtypeStruct((WEIGHT_ROWS, 2 * ADAPTER_RANK), jnp.float32),
            jax.ShapeDtypeStruct((ADAPTER_RANK, 2 * B_ROWS), jnp.float32),
        ),
        in_specs=[VMEM],
        out_specs=(VMEM, VMEM),
        scratch_shapes=[pltpu.VMEM((2 * ADAPTER_RANK, 2 * ADAPTER_RANK), jnp.float32)],
        compiler_params=PARAMS,
        name="term_sums",
    )(terms)


def token_gradients(query, kv_back, query_up, value_up):
    tokens = query.shape[0]
    return pl.pallas_call(
        token_kernel,
        out_shape=(
            jax.ShapeDtypeStruct((tokens, KEY_VALUE_HEADS * KV_COLS), jnp.bfloat16),
            jax.ShapeDtypeStruct((tokens, 2 * ADAPTER_RANK), jnp.bfloat16),
        ),
        in_specs=[VMEM] * 4,
        out_specs=(VMEM, VMEM),
        compiler_params=PARAMS,
        cost_estimate=pl.CostEstimate(
            flops=16 * 10**9, bytes_accessed=2 * 2**20, transcendentals=0
        ),
        name="token_gradients",
    )(query, kv_back, query_up, value_up)


def input_product(place, query, pairs, between, own, other):
    return pl.pallas_call(
        input_kernel,
        out_shape=jax.ShapeDtypeStruct((query.shape[0], MODEL_WIDTH), jnp.bfloat16),
        in_specs=[SMEM] + [VMEM] * 5,
        out_specs=VMEM,
        compiler_params=PARAMS,
        name="input_gradient",
    )(place, query, pairs, between, own, other)


def exchange(blocks, axes):
    return lax.all_to_all(blocks, axes, split_axis=0, concat_axis=0, tiled=True)


def swap(block):
    return lax.ppermute(block, "core", [(0, 1), (1, 0)])


def from_next(block):
    sections = lax.axis_size("section")
    return lax.ppermute(block, "section", [((i + 1) % sections, i) for i in range(sections)])


def along(block, distance):
    return lax.ppermute(block, "y", [(y, (y + distance) % LINE) for y in range(LINE)])


def by_source(pieces, line_at):
    doubled = jnp.stack(pieces[::-1] + pieces[:0:-1])
    return lax.dynamic_slice_in_dim(doubled, LINE - 1 - line_at, LINE, 0)


def core_order(own, other, core, axis):
    return jnp.stack(
        [jnp.where(core == 0, own, other), jnp.where(core == 0, other, own)], axis=axis
    )


def ordered(first, second):
    return lax.optimization_barrier((first, second))


def per_device(
    hidden,
    queries,
    keys_values,
    out_grad,
    qkv_weight,
    out_weight,
    adapter_down_maps,
    adapter_up_maps,
):
    line_at = lax.axis_index("y")
    core = lax.axis_index("core")
    place = jnp.stack([lax.axis_index("z"), core]).astype(jnp.int32)
    tokens = SEQS * PER_SEQ
    halves = LINE // SEQS
    qkv_cols = WEIGHT_COLS - 2 * ADAPTER_RANK

    kv_part = keys_values[0].reshape(SEQS, PER_SEQ, halves, CORES, KV_COLS).transpose(0, 2, 3, 1, 4)
    out_part = (
        out_weight[0]
        .reshape(WEIGHT_ROWS, halves, CORES, 2, GROUP_WIDTH // 2)
        .transpose(1, 2, 3, 0, 4)
        .reshape(1, halves, CORES, 2 * WEIGHT_ROWS, GROUP_WIDTH // 2)
    )
    group_send = jnp.concatenate(
        [kv_part, jnp.broadcast_to(out_part, (SEQS,) + out_part.shape[1:])], axis=3
    ).reshape(LINE * CORES, PER_SEQ + 2 * WEIGHT_ROWS, KV_COLS)
    group_line = exchange(group_send, ("y", "core"))

    grad_part = jnp.broadcast_to(out_grad[0][:, None], (SEQS, halves, PER_SEQ, MODEL_WIDTH))
    query_part = queries[0].reshape(SEQS, PER_SEQ, halves, PAIR_WIDTH).transpose(0, 2, 1, 3)
    kv_weight = (
        qkv_weight[0, :, Q_COLS:]
        .reshape(WEIGHT_ROWS, 2, KEY_VALUE_HEADS, HEAD_SIZE)
        .transpose(0, 2, 1, 3)
        .reshape(WEIGHT_ROWS, KEY_VALUE_HEADS * KV_COLS)
    )
    weights = jnp.concatenate(
        [qkv_weight[0, :, :Q_COLS], kv_weight, adapter_down_maps[0]], axis=1
    )
    folded = jnp.concatenate([weights[:, :FOLD], weights[:, WEIGHT_COLS - FOLD :]], axis=0)
    weight_part = jnp.broadcast_to(folded, (SEQS, halves, PER_SEQ, FOLD))
    row_send = jnp.concatenate([grad_part, query_part, weight_part], axis=3).reshape(
        LINE, PER_SEQ, ROW_COLS + FOLD
    )
    group_line, row_send = ordered(group_line, row_send)
    group_all = lax.all_gather(group_line, "z", axis=0).reshape(
        RING, LINE, CORES, PER_SEQ + 2 * WEIGHT_ROWS, KV_COLS
    )
    row_own = exchange(row_send, ("y",))
    row_other = swap(row_own)
    weight_line = jnp.concatenate(
        [
            row_own[:, :WEIGHT_ROWS, ROW_COLS:],
            row_own[:, WEIGHT_ROWS:, ROW_COLS + 2 * FOLD - WEIGHT_COLS :],
        ],
        axis=2,
    )
    group_all, weight_line = ordered(group_all, weight_line)
    weight_own = lax.all_gather(weight_line, "z", axis=0)

    query_gradient, kv_grad = attend(place, row_own, row_other, group_all)
    kv_back = exchange(kv_grad.reshape(DEVICES, PER_SEQ, KV_COLS), SEQ_AXES)

    query_chip = core_order(query_gradient[:, 0], swap(query_gradient[:, 1]), core, 1)
    query_sends = [
        lax.dynamic_index_in_dim(query_chip, (line_at + d) % LINE, 0, keepdims=False)
        for d in range(LINE)
    ]
    query_sends[0], weight_own = ordered(query_sends[0], weight_own)
    weight_other = swap(weight_own)
    query_back = by_source(
        query_sends[:1] + [along(query_sends[d], d) for d in range(1, LINE)], line_at
    )
    query_local = (
        query_back.reshape(SEQS, halves * CORES, PER_SEQ, GROUP_WIDTH)
        .transpose(0, 2, 1, 3)
        .reshape(tokens, Q_COLS)
    )
    up_maps = adapter_up_maps[0]
    query_up = jnp.pad(up_maps[:, :Q_COLS], ((0, ADAPTER_RANK), (0, 0)))
    value_up = jnp.pad(
        up_maps[:, Q_COLS:].reshape(ADAPTER_RANK, KEY_VALUE_HEADS, 1, HEAD_SIZE),
        ((ADAPTER_RANK, 0), (0, 0), (1, 0), (0, 0)),
    ).reshape(2 * ADAPTER_RANK, KEY_VALUE_HEADS * KV_COLS)
    kv_local, adapter_between = token_gradients(query_local, kv_back, query_up, value_up)
    input_gradient = input_product(
        place, query_local, kv_local, adapter_between, weight_own, weight_other
    )

    down_own, down_other = weight_own[..., qkv_cols:], weight_other[..., qkv_cols:]
    down_all = (
        core_order(down_own, down_other, core, 2)
        .transpose(1, 0, 2, 3, 4)
        .reshape(MODEL_WIDTH, 2 * ADAPTER_RANK)
    )

    hidden_rows = hidden[0].reshape(tokens, MODEL_WIDTH)
    adapter_reduced = dot(hidden_rows, down_all).astype(jnp.bfloat16)
    a_term = contract(hidden_rows, adapter_between, ((0,), (0,)))
    value_term = contract(kv_local, adapter_reduced[:, ADAPTER_RANK:], ((0,), (0,)))
    value_term = value_term.reshape(KEY_VALUE_HEADS, 2, HEAD_SIZE, ADAPTER_RANK)[:, 1]
    b_turned = jnp.concatenate(
        [
            contract(query_local, adapter_reduced[:, :ADAPTER_RANK], ((0,), (0,))),
            value_term.reshape(KEY_VALUE_HEADS * HEAD_SIZE, ADAPTER_RANK),
        ],
        axis=0,
    )
    a_send = a_term.reshape(LINE * RING, CORES, WEIGHT_ROWS, 2 * ADAPTER_RANK)
    b_send = b_turned.reshape(LINE * RING, CORES, 2, B_ROWS, ADAPTER_RANK)
    b_send = jnp.concatenate([b_send[:, :, 0], b_send[:, :, 1]], axis=3)
    term_send = jnp.concatenate([a_send, b_send], axis=2)
    kept = lax.dynamic_index_in_dim(term_send, core, 1, keepdims=False)
    given = lax.dynamic_index_in_dim(term_send, 1 - core, 1, keepdims=False)
    taken = swap(given)
    input_gradient, taken = ordered(input_gradient, taken)
    passed = from_next(input_gradient.reshape(1, SEQS, PER_SEQ, MODEL_WIDTH))
    term_chip = (kept + taken).astype(jnp.bfloat16)
    a_sum, b_sum = term_sums(exchange(term_chip, ("y", "z")))
    return (passed, a_sum[None], b_sum[None])


def solution(mesh):
    sections = mesh.shape["section"]
    fine = Mesh(mesh.devices.reshape(sections, LINE, RING, CORES), ("section",) + SEQ_AXES)
    return jax.shard_map(
        per_device,
        mesh=fine,
        in_specs=(
            P("section", None, SEQ_AXES, None),
            P("section", None, SEQ_AXES, None),
            P("section", None, SEQ_AXES, None),
            P("section", None, SEQ_AXES, None),
            P("section", SEQ_AXES, None),
            P("section", SEQ_AXES, None),
            P("section", SEQ_AXES, None),
            P("section", None, None),
        ),
        out_specs=(
            P("section", None, SEQ_AXES, None),
            P("section", SEQ_AXES, None),
            P("section", None, SEQ_AXES),
        ),
        check_vma=False,
    )
```
